32 devices in a mesh: chan: 8 (over z, y), ctx: 4 (over x, core).
Axes of the slice: x: 2, y: 2, z: 4, core: 2. Of those that a mesh axis runs over, the one named last changes fastest.
Arguments:
- key_proj: bfloat16 [4096, 4096], P('ctx', 'chan'), may hold values from -6 to 6
- value_proj: bfloat16 [4096, 4096], P('ctx', 'chan'), may hold values from -6 to 6
- query_proj: bfloat16 [4096, 4096], P('ctx', 'chan'), may hold values from -6 to 6
- short_filter: bfloat16 [3, 3, 4096], P(None, None, 'chan'), may hold values from -3.5 to 3.5
- decay_rate: float32 [16, 4096], P(None, 'chan'), may hold values from 0.00012207031 to 0.05
- residue: float32 [16, 4096], P(None, 'chan'), may hold values from -0.03 to 0.03
- skip_gain: float32 [4096], P('chan'), may hold values from -1 to 1
- out_weight: bfloat16 [4096, 4096], P('chan'), may hold values from -0.125 to 0.125
Outputs:
- block_out: bfloat16 [4096, 4096], P('ctx', 'chan')
The draws below stay inside these ranges and needn't reach their ends.
All inputs are finite; a program needn't handle non-finite values.
Results may differ from the reference program's by a relative error of at most 0.023.
Values may be sent and summed in bfloat16 or wider, within the bound.
A program may use at most 128 MiB of HBM per device.

```python
import math
import jax
import jax.numpy as jnp
from jax import lax

D = 4096
KS = 3
ORDER = 16
SEQ = 4096
N_CHAN = 8


def with_spikes(result, key, source, target, blocks, factor):
    owner, partner = [(jnp.arange(result.shape[dim]) // (result.shape[dim] // blocks)).reshape([-1 if axis == dim else 1 for axis in range(result.ndim)]) for dim in (source, target)]
    chosen = jax.random.permutation(key, blocks)[partner]
    strong = (owner == chosen) | (owner == (partner + blocks // 2) % blocks)
    return jnp.where(strong, factor * result, result)


def block_levels(stream_key, extent, cuts, low, top_value):
    level = 1.0
    for dim, shards_of in cuts:
        steps = jax.random.uniform(jax.random.fold_in(jax.random.fold_in(stream_key, 6), dim), (shards_of,), jnp.float32, low / len(cuts), top_value / len(cuts))
        level = level * jnp.repeat(jnp.exp(steps), extent[dim] // shards_of).reshape((-1,) + (1,) * (len(extent) - 1 - dim))
    return level


def normal_values(stream_key, extent, scale, reach, cuts=(), kind=jnp.bfloat16):
    values = jax.random.normal(stream_key, extent, jnp.float32) * scale
    if len(cuts) > 0:
        values = block_levels(stream_key, extent, cuts, -0.22, 0.18) * values
    return jnp.clip(values, min=-reach, max=reach).astype(kind)


def gaussian_with(stream_key, extent, scale, most, shards, heavy, dtype=jnp.bfloat16):
    entries = scale * jax.random.normal(stream_key, extent, jnp.float32)
    if shards:
        entries = entries * block_levels(stream_key, extent, shards, -0.22, 0.18)
    return jnp.clip(with_spikes(entries, jax.random.fold_in(stream_key, 3), *heavy), -most, most).astype(dtype)


def setup_inputs(seed: int = 0) -> dict:
    seeds = jax.random.split(jax.random.key(seed), 9)
    key_proj = normal_values(seeds[0], (SEQ, D), 1.0, 6.0, ((0, 4), (1, 8)))
    value_proj = normal_values(seeds[1], (SEQ, D), 1.0, 6.0, ((0, 4), (1, 8)))
    query_proj = normal_values(seeds[2], (SEQ, D), 1.0, 6.0, ((0, 4), (1, 8)))
    short_filter = normal_values(seeds[3], (3, KS, D), KS ** -0.5, 3.5, ((2, 8),))
    decay_rate = jnp.clip(jnp.exp(math.log(0.05) - 6.015181 * jax.random.uniform(seeds[4], (ORDER, D), jnp.float32) ** block_levels(seeds[4], (ORDER, D), ((1, 8),), -0.2, 0.2)), 0.00012207031, 0.05)
    residue = normal_values(seeds[5], (ORDER, D), 0.004, 0.03, ((1, 8),), jnp.float32)
    skip_gain = jnp.clip(jax.random.uniform(seeds[6], (D,), jnp.float32, -1.0, 1.0) * block_levels(seeds[6], (D,), ((0, 8),), -0.4, 0.0), -1.0, 1.0)
    out_weight = gaussian_with(seeds[7], (D, D), D ** -0.5, 0.125, ((0, 8),), (0, 1, 8, 2.0))
    return {"key_proj": key_proj, "value_proj": value_proj, "query_proj": query_proj, "short_filter": short_filter, "decay_rate": decay_rate, "residue": residue, "skip_gain": skip_gain, "out_weight": out_weight}


def short_conv(signal, filter_taps):
    tap_count = filter_taps.shape[0]
    length = signal.shape[0]
    padded = jnp.pad(signal, ((tap_count - 1, 0), (0, 0)))
    running = jnp.zeros(signal.shape, jnp.float32)
    for tap_index in range(tap_count):
        offset = tap_count - 1 - tap_index
        running = running + filter_taps[tap_index][None, :] * padded[offset:offset + length]
    return running


def modal_conv(signal, decay_rate, residue):
    channels, length = signal.shape
    tile_rows = 128
    blocks = length // tile_rows
    rates = decay_rate.T
    weights = residue.T
    position = jnp.arange(tile_rows).astype(jnp.float32)
    kernel = jnp.einsum('cm,cml->cl', weights, jnp.exp(-rates[:, :, None] * position[None, None, :]), precision=lax.Precision.HIGHEST)
    lag_index = jnp.arange(tile_rows)[:, None] - jnp.arange(tile_rows)[None, :]
    toeplitz = jnp.where(lag_index[None] >= 0, kernel[:, jnp.clip(lag_index, 0, tile_rows - 1)], jnp.float32(0.0))
    tiles = signal.reshape(channels, blocks, tile_rows)
    inside = jnp.einsum('cij,cnj->cni', toeplitz, tiles, precision=lax.Precision.HIGHEST)
    leaving = jnp.exp(-rates[:, :, None] * (tile_rows - position)[None, None, :])
    deposit = jnp.einsum('cmj,cnj->cnm', leaving, tiles, precision=lax.Precision.HIGHEST)
    factor = jnp.broadcast_to(jnp.exp(-rates * tile_rows)[:, None, :], deposit.shape)

    def combine(first, second):
        return (first[0] * second[0], first[1] * second[0] + second[1])

    _, ending = lax.associative_scan(combine, (factor, deposit), axis=1)
    starting = jnp.concatenate([jnp.zeros_like(ending[:, :1]), ending[:, :-1]], 1)
    arriving = weights[:, :, None] * jnp.exp(-rates[:, :, None] * position[None, None, :])
    carried = jnp.einsum('cnm,cmi->cni', starting, arriving, precision=lax.Precision.HIGHEST)
    return (inside + carried).reshape(channels, length), ending[:, -1]


def regroup(array_in):
    return array_in.reshape(array_in.shape[0], N_CHAN, -1).transpose(1, 0, 2)


def reference(key_proj, value_proj, query_proj, short_filter, decay_rate, residue, skip_gain, out_weight):
    filter_groups = short_filter.reshape(3, KS, N_CHAN, -1).transpose(2, 0, 1, 3)

    def per_group(inputs_group):
        key_group, value_group, query_group, filter_group, rate_group, residue_group, skip_group = inputs_group
        taps = filter_group.astype(jnp.float32)
        feat_query = short_conv(query_group.astype(jnp.float32), taps[0])
        feat_key = short_conv(key_group.astype(jnp.float32), taps[1])
        feat_value = short_conv(value_group.astype(jnp.float32), taps[2])
        product = (feat_key * feat_value).astype(jnp.bfloat16)
        signal = product.T.astype(jnp.float32)
        conv, _ = modal_conv(signal, rate_group, residue_group)
        long_out = (conv + skip_group[:, None] * signal).astype(jnp.bfloat16).T
        return (feat_query * long_out.astype(jnp.float32)).astype(jnp.bfloat16)

    grouped = lax.map(per_group, (regroup(key_proj), regroup(value_proj), regroup(query_proj), filter_groups, regroup(decay_rate), regroup(residue), skip_gain.reshape(N_CHAN, -1)))
    weight_groups = out_weight.reshape(N_CHAN, -1, D)

    def accumulate(running, operands):
        partial_sum = jnp.dot(operands[0], operands[1], preferred_element_type=jnp.float32).astype(jnp.bfloat16)
        return running + partial_sum.astype(jnp.float32), None

    summed, _ = lax.scan(accumulate, jnp.zeros((SEQ, D), jnp.float32), (grouped, weight_groups))
    return summed.astype(jnp.bfloat16)
```

```python
import functools

import jax
import jax.numpy as jnp
from jax import lax
from jax.experimental import pallas as pl
from jax.experimental.pallas import tpu as pltpu
from jax.sharding import PartitionSpec as P

MESH = pl.DeviceIdType.MESH
LANES = 128
SUB = 8
PAD = 16
INNER = 2
F32 = jnp.float32
BF16 = jnp.bfloat16


def kernel(
    n_chan, n_ctx, chunks,
    k_hbm, v_hbm, q_hbm, taps_ref, decay_ref, residue_ref, skip_ref, w_hbm,
    out_ref,
    kpad, vpad, qpad, prod, conv, amp, weight, states, ending, arrived, entering,
    gated, wbuf, from_left, from_right, acc,
    in_sem, halo_send, halo_recv, wl_sem, wy_send, wy_recv, wr_send, wr_recv,
    st_send, st_recv, g_send, g_recv, l_send, l_recv, r_send, r_recv,
):
    rows, width = k_hbm.shape
    modes = decay_ref.shape[0]
    depth = w_hbm.shape[0]
    half = depth // 2
    line = n_chan // INNER
    chunk = rows // chunks
    seg = chunk // SUB
    block = modes * SUB
    groups = width // LANES

    chan = lax.axis_index("chan")
    ctx = lax.axis_index("ctx")
    z = chan // INNER
    y = chan % INNER
    core = ctx % 2
    peer = {"chan": z * INNER + (1 - y), "ctx": ctx}
    mate = {"chan": chan, "ctx": ctx + 1 - 2 * core}
    left = {"chan": chan - INNER, "ctx": ctx}
    right = {"chan": chan + INNER, "ctx": ctx}

    barrier = pltpu.get_barrier_semaphore()

    def greet(device):
        pl.semaphore_signal(barrier, inc=1, device_id=device, device_id_type=MESH)

    @pl.loop(0, n_ctx)
    def _(i):
        @pl.when(i != ctx)
        def _():
            greet({"chan": chan, "ctx": i})

    greet(peer)

    @pl.when(z > 0)
    def _():
        greet(left)

    @pl.when(z < line - 1)
    def _():
        greet(right)

    pads = ((k_hbm, kpad), (v_hbm, vpad), (q_hbm, qpad))
    loads = [
        pltpu.make_async_copy(src, dst.at[pl.ds(PAD, rows)], in_sem.at[i])
        for i, (src, dst) in enumerate(pads)
    ]
    for load in loads:
        load.start()

    def own_w(d):
        cols = pl.ds(pl.multiple_of((d * INNER + y) * width, LANES), width)
        return pltpu.make_async_copy(w_hbm.at[:, cols], wbuf.at[0, d], wl_sem.at[d])

    @pl.loop(0, line)
    def _(d):
        own_w(d).start()

    has_left = (z + line - 1) // line
    has_right = (2 * line - 2 - z) // line
    pl.semaphore_wait(barrier, n_ctx + has_left + has_right)

    def halo(i):
        src, dst = pads[i]
        return pltpu.make_async_remote_copy(
            src_ref=src.at[pl.ds(rows - PAD, PAD)],
            dst_ref=dst.at[pl.ds(0, PAD)],
            send_sem=halo_send.at[i],
            recv_sem=halo_recv.at[i],
            device_id={"chan": chan, "ctx": ctx + 1},
            device_id_type=MESH,
        )

    @pl.when(ctx < n_ctx - 1)
    def _():
        for i in range(3):
            halo(i).start()

    @pl.when(ctx == 0)
    def _():
        for _, dst in pads:
            dst[pl.ds(0, PAD), :] = jnp.zeros((PAD, width), BF16)

    mine = pl.ds(pl.multiple_of(core * half, PAD), half)

    def piece(o):
        return jnp.where(o % 2 == 0, line - 1 - o // 2, o // 2)

    def cross_w(d):
        cols = pl.ds(pl.multiple_of((d * INNER + 1 - y) * width, LANES), width)
        return pltpu.make_async_remote_copy(
            src_ref=w_hbm.at[mine, cols],
            dst_ref=wbuf.at[1, d, mine],
            send_sem=wy_send.at[d],
            recv_sem=wy_recv.at[d],
            device_id=peer,
            device_id_type=MESH,
        )

    def relay_w(d):
        return pltpu.make_async_remote_copy(
            src_ref=wbuf.at[1, d, mine],
            dst_ref=wbuf.at[1, d, mine],
            send_sem=wr_send.at[d],
            recv_sem=wr_recv.at[d],
            device_id=mate,
            device_id_type=MESH,
        )

    @pl.loop(0, line)
    def _(o):
        cross_w(piece(o)).start()

    amp[...] = jnp.broadcast_to(jnp.exp(-decay_ref[...])[:, None, :], amp.shape)
    weight[...] = jnp.broadcast_to(residue_ref[...][:, None, :], weight.shape)

    for load in loads:
        load.wait()

    @pl.when(ctx > 0)
    def _():
        for i in range(3):
            halo(i).wait_recv()

    def featurize(pad, branch, start, count, lanes):
        window = pad[pl.ds(start, count + PAD), lanes].astype(F32)
        taps = taps_ref[branch, :, lanes].astype(F32)
        feat = taps[0:1] * window[PAD:]
        for lag in range(1, taps.shape[0]):
            feat = feat + taps[lag : lag + 1] * pltpu.roll(window, lag, 0)[PAD:]
        return feat

    feat_rows = min(128, rows)

    def lane_slice(g):
        return pl.ds(pl.multiple_of(g * LANES, LANES), LANES)

    @pl.loop(0, groups)
    def _(g):
        lanes = lane_slice(g)

        @pl.loop(0, rows // feat_rows)
        def _(b):
            start = pl.multiple_of(b * feat_rows, feat_rows)
            product = featurize(kpad, 1, start, feat_rows, lanes) * featurize(
                vpad, 2, start, feat_rows, lanes
            )
            prod[g, pl.ds(start, feat_rows), :] = product.astype(BF16).astype(F32)

        a = amp[:, :, lanes]

        @pl.loop(0, chunks)
        def _(c):
            def step(i, state):
                for u in range(SUB):
                    p = prod[g, pl.ds(c * chunk + i * SUB + u, SUB, stride=seg), :]
                    state = a * state + p[None]
                return state

            state = lax.fori_loop(0, seg // SUB, step, jnp.zeros((modes, SUB, LANES), F32))
            states[g, pl.ds(pl.multiple_of(c * block, block), block), :] = state.reshape(block, LANES)

    def segment(g, c, s):
        return states.at[g, pl.ds(c * block + s, modes, stride=SUB), :]

    @pl.loop(0, groups)
    def _(g):
        lanes = lane_slice(g)
        factor = jnp.exp(-decay_ref[:, lanes] * seg)

        def step(c, state):
            for s in range(SUB):
                state = factor * state + segment(g, c, s)[...]
            return state

        ending[:, lanes] = lax.fori_loop(0, chunks, step, jnp.zeros((modes, LANES), F32))

    def state_copy(source, target):
        return pltpu.make_async_remote_copy(
            src_ref=ending,
            dst_ref=arrived.at[source],
            send_sem=st_send.at[target],
            recv_sem=st_recv.at[source],
            device_id={"chan": chan, "ctx": target},
            device_id_type=MESH,
        )

    @pl.loop(0, n_ctx)
    def _(i):
        @pl.when(i > ctx)
        def _():
            state_copy(ctx, i).start()

    entering[...] = jnp.zeros_like(entering)

    @pl.loop(0, n_ctx)
    def _(j):
        @pl.when(j < ctx)
        def _():
            state_copy(j, ctx).wait_recv()
            entering[...] = entering[...] * jnp.exp(-decay_ref[...] * rows) + arrived[j]

    @pl.loop(0, groups)
    def _(g):
        lanes = lane_slice(g)
        factor = jnp.exp(-decay_ref[:, lanes] * seg)

        def step(c, state):
            for s in range(SUB):
                place = segment(g, c, s)
                later = factor * state + place[...]
                place[...] = state
                state = later
            return state

        lax.fori_loop(0, chunks, step, entering[:, lanes])

    def send_gated(c):
        part = pl.ds(pl.multiple_of(c * chunk, chunk), chunk)
        return pltpu.make_async_remote_copy(
            src_ref=gated.at[0, part],
            dst_ref=gated.at[1, part],
            send_sem=g_send.at[c],
            recv_sem=g_recv.at[c],
            device_id=peer,
            device_id_type=MESH,
        )

    gate_rows = min(128, chunk)

    @pl.loop(0, chunks)
    def _(c):
        @pl.loop(0, groups)
        def _(g):
            lanes = lane_slice(g)
            a = amp[:, :, lanes]
            r = weight[:, :, lanes]
            state = states[g, pl.ds(pl.multiple_of(c * block, block), block), :]

            def step(i, state):
                for u in range(SUB):
                    here = i * SUB + u
                    p = prod[g, pl.ds(c * chunk + here, SUB, stride=seg), :]
                    state = a * state + p[None]
                    conv[pl.ds(here, SUB, stride=seg), :] = jnp.sum(r * state, axis=0)
                return state

            lax.fori_loop(0, seg // SUB, step, state.reshape(modes, SUB, LANES))

            @pl.loop(0, chunk // gate_rows)
            def _(b):
                start = pl.multiple_of(c * chunk + b * gate_rows, gate_rows)
                inside = pl.ds(pl.multiple_of(b * gate_rows, gate_rows), gate_rows)
                here = pl.ds(start, gate_rows)
                long_out = conv[inside, :] + skip_ref[:, lanes] * prod[g, here, :]
                gate = featurize(qpad, 0, start, gate_rows, lanes)
                gated[0, here, lanes] = (gate * long_out.astype(BF16).astype(F32)).astype(BF16)

        send_gated(c).start()
        share = -(-line // chunks)
        for t in range(share):
            o = c * share + t

            @pl.when(o < line)
            def _():
                cross_w(piece(o)).wait_recv()
                relay_w(piece(o)).start()

    @pl.loop(0, line)
    def _(d):
        own_w(d).wait()
        relay_w(d).wait_recv()

    def hop(slots, send, recv, d, c, device):
        part = pl.ds(pl.multiple_of(c * chunk, chunk), chunk)
        return pltpu.make_async_remote_copy(
            src_ref=slots.at[d, part],
            dst_ref=slots.at[d, part],
            send_sem=send.at[d, c],
            recv_sem=recv.at[d, c],
            device_id=device,
            device_id_type=MESH,
        )

    def to_right(d, c):
        return hop(from_left, l_send, l_recv, d, c, right)

    def to_left(d, c):
        return hop(from_right, r_send, r_recv, d, c, left)

    def partial(d, part):
        acc[...] = jnp.dot(
            gated[0, part, :], wbuf[0, d], preferred_element_type=F32
        ) + jnp.dot(gated[1, part, :], wbuf[1, d], preferred_element_type=F32)

    def passed(slots, copy, first, d, c, part):
        partial(d, part)

        @pl.when(first)
        def _():
            slots[d, part, :] = acc[...].astype(BF16)

        @pl.when(jnp.logical_not(first))
        def _():
            copy.wait_recv()
            slots[d, part, :] = (acc[...] + slots[d, part, :].astype(F32)).astype(BF16)

        copy.start()

    @pl.loop(0, chunks)
    def _(c):
        part = pl.ds(pl.multiple_of(c * chunk, chunk), chunk)
        send_gated(c).wait_recv()

        @pl.loop(0, line - 1)
        def _(s):
            far = line - 1 - s

            @pl.when(far > z)
            def _():
                passed(from_left, to_right(far, c), z == 0, far, c, part)

            @pl.when(s < z)
            def _():
                passed(from_right, to_left(s, c), z == line - 1, s, c, part)

        partial(z, part)

        @pl.when(z > 0)
        def _():
            to_right(z, c).wait_recv()
            acc[...] += from_left[z, part, :].astype(F32)

        @pl.when(z < line - 1)
        def _():
            to_left(z, c).wait_recv()
            acc[...] += from_right[z, part, :].astype(F32)

        out_ref[part, :] = acc[...].astype(BF16)

    @pl.when(ctx < n_ctx - 1)
    def _():
        for i in range(3):
            halo(i).wait_send()

    @pl.loop(0, n_ctx)
    def _(i):
        @pl.when(i > ctx)
        def _():
            state_copy(ctx, i).wait_send()

    @pl.loop(0, chunks)
    def _(c):
        send_gated(c).wait_send()

    @pl.loop(0, line)
    def _(d):
        cross_w(d).wait_send()
        relay_w(d).wait_send()

        @pl.loop(0, chunks)
        def _(c):
            @pl.when(d > z)
            def _():
                to_right(d, c).wait_send()

            @pl.when(d < z)
            def _():
                to_left(d, c).wait_send()


def local(mesh, chunks, key_proj, value_proj, query_proj, short_filter, decay_rate, residue, skip_gain, out_weight):
    n_chan, n_ctx = mesh.shape["chan"], mesh.shape["ctx"]
    rows, width = key_proj.shape
    modes = decay_rate.shape[0]
    depth = out_weight.shape[0]
    line = n_chan // INNER
    chunk = rows // chunks
    groups = width // LANES
    dma = pltpu.SemaphoreType.DMA
    vmem = pl.BlockSpec(memory_space=pltpu.VMEM)
    hbm = pl.BlockSpec(memory_space=pl.ANY)
    return pl.pallas_call(
        functools.partial(kernel, n_chan, n_ctx, chunks),
        out_shape=jax.ShapeDtypeStruct((rows, width), BF16),
        in_specs=[hbm, hbm, hbm, vmem, vmem, vmem, vmem, hbm],
        out_specs=vmem,
        scratch_shapes=[
            pltpu.VMEM((rows + PAD, width), BF16),
            pltpu.VMEM((rows + PAD, width), BF16),
            pltpu.VMEM((rows + PAD, width), BF16),
            pltpu.VMEM((groups, rows, LANES), F32),
            pltpu.VMEM((chunk, LANES), F32),
            pltpu.VMEM((modes, SUB, width), F32),
            pltpu.VMEM((modes, SUB, width), F32),
            pltpu.VMEM((groups, chunks * modes * SUB, LANES), F32),
            pltpu.VMEM((modes, width), F32),
            pltpu.VMEM((n_ctx, modes, width), F32),
            pltpu.VMEM((modes, width), F32),
            pltpu.VMEM((2, rows, width), BF16),
            pltpu.VMEM((2, line, depth, width), BF16),
            pltpu.VMEM((line, rows, width), BF16),
            pltpu.VMEM((line, rows, width), BF16),
            pltpu.VMEM((chunk, width), F32),
            dma((3,)), dma((3,)), dma((3,)),
            dma((line,)), dma((line,)), dma((line,)), dma((line,)), dma((line,)),
            dma((n_ctx,)), dma((n_ctx,)),
            dma((chunks,)), dma((chunks,)),
            dma((line, chunks)), dma((line, chunks)),
            dma((line, chunks)), dma((line, chunks)),
        ],
        compiler_params=pltpu.CompilerParams(
            collective_id=0, has_side_effects=True, vmem_limit_bytes=48 * 1024 * 1024
        ),
    )(
        key_proj, value_proj, query_proj, short_filter, decay_rate, residue,
        skip_gain.reshape(1, width), out_weight,
    )


def solution(mesh):
    placed = (
        P("ctx", "chan"),
        P("ctx", "chan"),
        P("ctx", "chan"),
        P(None, None, "chan"),
        P(None, "chan"),
        P(None, "chan"),
        P("chan"),
        P("chan", None),
    )
    return jax.shard_map(
        functools.partial(local, mesh, 4),
        mesh=mesh, in_specs=placed, out_specs=P("ctx", "chan"), check_vma=False,
    )
```

```python
import functools

import jax
import jax.numpy as jnp
from jax import lax
from jax.experimental import pallas as pl
from jax.experimental.pallas import tpu as pltpu
from jax.sharding import PartitionSpec as P

MESH = pl.DeviceIdType.MESH
LANES = 128
SUB = 8
PAD = 16
INNER = 2
FLIGHT = 2
EARLY = 0
F32 = jnp.float32
BF16 = jnp.bfloat16


def kernel(
    n_chan, n_ctx, chunks,
    k_hbm, v_hbm, q_hbm, taps_ref, decay_ref, residue_ref, skip_ref, w_hbm,
    out_ref,
    kpad, vpad, qpad, prod, conv, amp, weight, states, ending, arrived, entering,
    gated, wbuf, from_left, from_right, acc, own,
    in_sem, halo_send, halo_recv, wl_sem, wy_send, wy_recv, wr_send, wr_recv,
    st_send, st_recv, g_send, g_recv, l_send, l_recv, r_send, r_recv,
):
    rows, width = k_hbm.shape
    modes = decay_ref.shape[0]
    depth = w_hbm.shape[0]
    half = depth // 2
    line = n_chan // INNER
    chunk = rows // chunks
    seg = chunk // SUB
    block = modes * SUB
    groups = width // LANES

    chan = lax.axis_index("chan")
    ctx = lax.axis_index("ctx")
    z = chan // INNER
    y = chan % INNER
    core = ctx % 2
    peer = {"chan": z * INNER + (1 - y), "ctx": ctx}
    mate = {"chan": chan, "ctx": ctx + 1 - 2 * core}
    left = {"chan": chan - INNER, "ctx": ctx}
    right = {"chan": chan + INNER, "ctx": ctx}

    barrier = pltpu.get_barrier_semaphore()

    def greet(device):
        pl.semaphore_signal(barrier, inc=1, device_id=device, device_id_type=MESH)

    @pl.loop(0, n_ctx)
    def _(i):
        @pl.when(i != ctx)
        def _():
            greet({"chan": chan, "ctx": i})

    greet(peer)

    @pl.when(z > 0)
    def _():
        greet(left)

    @pl.when(z < line - 1)
    def _():
        greet(right)

    pads = ((k_hbm, kpad), (v_hbm, vpad), (q_hbm, qpad))
    loads = [
        pltpu.make_async_copy(src, dst.at[pl.ds(PAD, rows)], in_sem.at[i])
        for i, (src, dst) in enumerate(pads)
    ]
    for load in loads:
        load.start()

    def own_w(d):
        cols = pl.ds(pl.multiple_of((d * INNER + y) * width, LANES), width)
        return pltpu.make_async_copy(w_hbm.at[:, cols], wbuf.at[0, d], wl_sem.at[d])

    @pl.loop(0, line)
    def _(d):
        own_w(d).start()

    has_left = (z + line - 1) // line
    has_right = (2 * line - 2 - z) // line
    pl.semaphore_wait(barrier, n_ctx + has_left + has_right)

    def halo(i):
        src, dst = pads[i]
        return pltpu.make_async_remote_copy(
            src_ref=src.at[pl.ds(rows - PAD, PAD)],
            dst_ref=dst.at[pl.ds(0, PAD)],
            send_sem=halo_send.at[i],
            recv_sem=halo_recv.at[i],
            device_id={"chan": chan, "ctx": ctx + 1},
            device_id_type=MESH,
        )

    @pl.when(ctx < n_ctx - 1)
    def _():
        for i in range(3):
            halo(i).start()

    @pl.when(ctx == 0)
    def _():
        for _, dst in pads:
            dst[pl.ds(0, PAD), :] = jnp.zeros((PAD, width), BF16)

    mine = pl.ds(pl.multiple_of(core * half, PAD), half)

    half_line = max(line // 2, 1)
    upper = z // half_line

    def piece(o):
        d = jnp.where(o % 2 == 0, line - 1 - o // 2, o // 2)
        return jnp.where(upper == 1, line - 1 - d, d)

    def order_of(d):
        d = jnp.where(upper == 1, line - 1 - d, d)
        return jnp.where(d >= half_line, 2 * (line - 1 - d), 2 * d + 1)

    def cross_w(d):
        cols = pl.ds(pl.multiple_of((d * INNER + 1 - y) * width, LANES), width)
        return pltpu.make_async_remote_copy(
            src_ref=w_hbm.at[mine, cols],
            dst_ref=wbuf.at[1, d, mine],
            send_sem=wy_send.at[d],
            recv_sem=wy_recv.at[d],
            device_id=peer,
            device_id_type=MESH,
        )

    def relay_w(d):
        return pltpu.make_async_remote_copy(
            src_ref=wbuf.at[1, d, mine],
            dst_ref=wbuf.at[1, d, mine],
            send_sem=wr_send.at[d],
            recv_sem=wr_recv.at[d],
            device_id=mate,
            device_id_type=MESH,
        )

    early = line // 2 + EARLY

    @pl.loop(0, early)
    def _(o):
        cross_w(piece(o)).start()

    amp[...] = jnp.broadcast_to(jnp.exp(-decay_ref[...])[:, None, :], amp.shape)
    weight[...] = jnp.broadcast_to(residue_ref[...][:, None, :], weight.shape)

    for load in loads:
        load.wait()

    @pl.when(ctx > 0)
    def _():
        for i in range(3):
            halo(i).wait_recv()

    def featurize(pad, branch, start, count, lanes):
        window = pad[pl.ds(start, count + PAD), lanes].astype(F32)
        taps = taps_ref[branch, :, lanes].astype(F32)
        feat = taps[0:1] * window[PAD:]
        for lag in range(1, taps.shape[0]):
            feat = feat + taps[lag : lag + 1] * pltpu.roll(window, lag, 0)[PAD:]
        return feat

    feat_rows = min(128, rows)

    def lane_slice(g):
        return pl.ds(pl.multiple_of(g * LANES, LANES), LANES)

    @pl.loop(0, groups)
    def _(g):
        lanes = lane_slice(g)

        @pl.loop(0, rows // feat_rows)
        def _(b):
            start = pl.multiple_of(b * feat_rows, feat_rows)
            product = featurize(kpad, 1, start, feat_rows, lanes) * featurize(
                vpad, 2, start, feat_rows, lanes
            )
            prod[g, pl.ds(start, feat_rows), :] = product.astype(BF16).astype(F32)

        a = amp[:, :, lanes]

        @pl.loop(0, chunks)
        def _(c):
            def step(i, state):
                for u in range(SUB):
                    p = prod[g, pl.ds(c * chunk + i * SUB + u, SUB, stride=seg), :]
                    state = a * state + p[None]
                return state

            state = lax.fori_loop(0, seg // SUB, step, jnp.zeros((modes, SUB, LANES), F32))
            states[g, pl.ds(pl.multiple_of(c * block, block), block), :] = state.reshape(block, LANES)

    def segment(g, c, s):
        return states.at[g, pl.ds(c * block + s, modes, stride=SUB), :]

    @pl.loop(0, groups)
    def _(g):
        lanes = lane_slice(g)
        factor = jnp.exp(-decay_ref[:, lanes] * seg)

        def step(c, state):
            for s in range(SUB):
                state = factor * state + segment(g, c, s)[...]
            return state

        ending[:, lanes] = lax.fori_loop(0, chunks, step, jnp.zeros((modes, LANES), F32))

    def state_copy(source, target):
        return pltpu.make_async_remote_copy(
            src_ref=ending,
            dst_ref=arrived.at[source],
            send_sem=st_send.at[target],
            recv_sem=st_recv.at[source],
            device_id={"chan": chan, "ctx": target},
            device_id_type=MESH,
        )

    @pl.loop(0, n_ctx)
    def _(i):
        @pl.when(i > ctx)
        def _():
            state_copy(ctx, i).start()

    entering[...] = jnp.zeros_like(entering)

    @pl.loop(0, n_ctx)
    def _(j):
        @pl.when(j < ctx)
        def _():
            state_copy(j, ctx).wait_recv()
            entering[...] = entering[...] * jnp.exp(-decay_ref[...] * rows) + arrived[j]

    @pl.loop(0, groups)
    def _(g):
        lanes = lane_slice(g)
        factor = jnp.exp(-decay_ref[:, lanes] * seg)

        def step(c, state):
            for s in range(SUB):
                place = segment(g, c, s)
                later = factor * state + place[...]
                place[...] = state
                state = later
            return state

        lax.fori_loop(0, chunks, step, entering[:, lanes])

    def send_gated(c):
        part = pl.ds(pl.multiple_of(c * chunk, chunk), chunk)
        return pltpu.make_async_remote_copy(
            src_ref=gated.at[0, part],
            dst_ref=gated.at[1, part],
            send_sem=g_send.at[c],
            recv_sem=g_recv.at[c],
            device_id=peer,
            device_id_type=MESH,
        )

    gate_rows = min(128, chunk)

    @pl.loop(0, chunks)
    def _(c):
        @pl.loop(0, groups)
        def _(g):
            lanes = lane_slice(g)
            a = amp[:, :, lanes]
            r = weight[:, :, lanes]
            state = states[g, pl.ds(pl.multiple_of(c * block, block), block), :]

            def step(i, state):
                for u in range(SUB):
                    here = i * SUB + u
                    p = prod[g, pl.ds(c * chunk + here, SUB, stride=seg), :]
                    state = a * state + p[None]
                    conv[pl.ds(here, SUB, stride=seg), :] = jnp.sum(r * state, axis=0)
                return state

            lax.fori_loop(0, seg // SUB, step, state.reshape(modes, SUB, LANES))

            @pl.loop(0, chunk // gate_rows)
            def _(b):
                start = pl.multiple_of(c * chunk + b * gate_rows, gate_rows)
                inside = pl.ds(pl.multiple_of(b * gate_rows, gate_rows), gate_rows)
                here = pl.ds(start, gate_rows)
                long_out = conv[inside, :] + skip_ref[:, lanes] * prod[g, here, :]
                gate = featurize(qpad, 0, start, gate_rows, lanes)
                gated[0, here, lanes] = (gate * long_out.astype(BF16).astype(F32)).astype(BF16)

        @pl.when(c == 0)
        def _():
            send_gated(c).start()

    @pl.loop(0, early)
    def _(o):
        cross_w(piece(o)).wait_recv()
        relay_w(piece(o)).start()

    @pl.loop(0, line)
    def _(d):
        own_w(d).wait()

    def ready_w(d):
        @pl.when(order_of(d) >= early)
        def _():
            cross_w(d).wait_recv()
            relay_w(d).start()

        relay_w(d).wait_recv()

    def hop(slots, send, recv, d, c, device):
        part = pl.ds(pl.multiple_of(c * chunk, chunk), chunk)
        return pltpu.make_async_remote_copy(
            src_ref=slots.at[d, part],
            dst_ref=slots.at[d, part],
            send_sem=send.at[d, c],
            recv_sem=recv.at[d, c],
            device_id=device,
            device_id_type=MESH,
        )

    def to_right(d, c):
        return hop(from_left, l_send, l_recv, d, c, right)

    def to_left(d, c):
        return hop(from_right, r_send, r_recv, d, c, left)

    def partial(d, c, part):
        @pl.when(c == 0)
        def _():
            ready_w(d)

        return jnp.dot(
            gated[0, part, :], wbuf[0, d], preferred_element_type=F32
        ) + jnp.dot(gated[1, part, :], wbuf[1, d], preferred_element_type=F32)

    def passed(slots, copy, earlier, begins, starts, d, c, part):
        acc[...] = partial(d, c, part)

        @pl.when(begins)
        def _():
            slots[d, part, :] = acc[...].astype(BF16)

        @pl.when(jnp.logical_not(begins))
        def _():
            copy(d, c).wait_recv()
            slots[d, part, :] = (acc[...] + slots[d, part, :].astype(F32)).astype(BF16)

        @pl.when(jnp.logical_not(starts))
        def _():
            earlier(d, c, FLIGHT).wait_send()

        copy(d, c).start()

    def earlier_right(d, c, steps):
        for _ in range(steps):
            new = d == line - 1
            d, c = jnp.where(new, z + 1, d + 1), jnp.where(new, c - 1, c)
        return to_right(d, c)

    def earlier_left(d, c, steps):
        for _ in range(steps):
            new = d == 0
            d, c = jnp.where(new, z - 1, d - 1), jnp.where(new, c - 1, c)
        return to_left(d, c)

    @pl.loop(0, chunks)
    def _(c):
        part = pl.ds(pl.multiple_of(c * chunk, chunk), chunk)

        send_gated(c).wait_recv()

        @pl.when(c == 0)
        def _():
            @pl.loop(early, line)
            def _(o):
                cross_w(piece(o)).start()

        @pl.when(c < chunks - 1)
        def _():
            send_gated(c + 1).start()

        def rightward(s):
            far = line - 1 - s

            @pl.when(far > z)
            def _():
                starts = c * (line - 1 - z) + s < FLIGHT
                passed(from_left, to_right, earlier_right, z == 0, starts, far, c, part)

        def leftward(s):
            @pl.when(s < z)
            def _():
                starts = c * z + s < FLIGHT
                passed(from_right, to_left, earlier_left, z == line - 1, starts, s, c, part)

        @pl.loop(0, line - 1)
        def _(s):
            @pl.when(upper == 0)
            def _():
                rightward(s)
                leftward(s)

            @pl.when(upper > 0)
            def _():
                leftward(s)
                rightward(s)

        own[part, :] = partial(z, c, part)

    @pl.loop(0, chunks)
    def _(c):
        part = pl.ds(pl.multiple_of(c * chunk, chunk), chunk)

        @pl.when(z > 0)
        def _():
            to_right(z, c).wait_recv()
            own[part, :] += from_left[z, part, :].astype(F32)

        @pl.when(z < line - 1)
        def _():
            to_left(z, c).wait_recv()
            own[part, :] += from_right[z, part, :].astype(F32)

        out_ref[part, :] = own[part, :].astype(BF16)

    @pl.when(ctx < n_ctx - 1)
    def _():
        for i in range(3):
            halo(i).wait_send()

    @pl.loop(0, n_ctx)
    def _(i):
        @pl.when(i > ctx)
        def _():
            state_copy(ctx, i).wait_send()

    @pl.loop(0, chunks)
    def _(c):
        send_gated(c).wait_send()

    @pl.loop(0, line)
    def _(d):
        cross_w(d).wait_send()
        relay_w(d).wait_send()

    @pl.when(z < line - 1)
    def _():
        for steps in range(FLIGHT):
            earlier_right(z + 1, chunks - 1, steps).wait_send()

    @pl.when(z > 0)
    def _():
        for steps in range(FLIGHT):
            earlier_left(z - 1, chunks - 1, steps).wait_send()


def local(mesh, chunks, key_proj, value_proj, query_proj, short_filter, decay_rate, residue, skip_gain, out_weight):
    n_chan, n_ctx = mesh.shape["chan"], mesh.shape["ctx"]
    rows, width = key_proj.shape
    modes = decay_rate.shape[0]
    depth = out_weight.shape[0]
    line = n_chan // INNER
    chunk = rows // chunks
    groups = width // LANES
    dma = pltpu.SemaphoreType.DMA
    vmem = pl.BlockSpec(memory_space=pltpu.VMEM)
    hbm = pl.BlockSpec(memory_space=pl.ANY)
    return pl.pallas_call(
        functools.partial(kernel, n_chan, n_ctx, chunks),
        out_shape=jax.ShapeDtypeStruct((rows, width), BF16),
        in_specs=[hbm, hbm, hbm, vmem, vmem, vmem, vmem, hbm],
        out_specs=vmem,
        scratch_shapes=[
            pltpu.VMEM((rows + PAD, width), BF16),
            pltpu.VMEM((rows + PAD, width), BF16),
            pltpu.VMEM((rows + PAD, width), BF16),
            pltpu.VMEM((groups, rows, LANES), F32),
            pltpu.VMEM((chunk, LANES), F32),
            pltpu.VMEM((modes, SUB, width), F32),
            pltpu.VMEM((modes, SUB, width), F32),
            pltpu.VMEM((groups, chunks * modes * SUB, LANES), F32),
            pltpu.VMEM((modes, width), F32),
            pltpu.VMEM((n_ctx, modes, width), F32),
            pltpu.VMEM((modes, width), F32),
            pltpu.VMEM((2, rows, width), BF16),
            pltpu.VMEM((2, line, depth, width), BF16),
            pltpu.VMEM((line, rows, width), BF16),
            pltpu.VMEM((line, rows, width), BF16),
            pltpu.VMEM((chunk, width), F32),
            pltpu.VMEM((rows, width), F32),
            dma((3,)), dma((3,)), dma((3,)),
            dma((line,)), dma((line,)), dma((line,)), dma((line,)), dma((line,)),
            dma((n_ctx,)), dma((n_ctx,)),
            dma((chunks,)), dma((chunks,)),
            dma((line, chunks)), dma((line, chunks)),
            dma((line, chunks)), dma((line, chunks)),
        ],
        compiler_params=pltpu.CompilerParams(
            collective_id=0, has_side_effects=True, vmem_limit_bytes=60 * 1024 * 1024
        ),
    )(
        key_proj, value_proj, query_proj, short_filter, decay_rate, residue,
        skip_gain.reshape(1, width), out_weight,
    )


def solution(mesh):
    placed = (
        P("ctx", "chan"),
        P("ctx", "chan"),
        P("ctx", "chan"),
        P(None, None, "chan"),
        P(None, "chan"),
        P(None, "chan"),
        P("chan"),
        P("chan", None),
    )
    return jax.shard_map(
        functools.partial(local, mesh, 4),
        mesh=mesh, in_specs=placed, out_specs=P("ctx", "chan"), check_vma=False,
    )
```
